32 devices in a mesh: groups: 2 (over y), tiles: 4 (over z), cols: 2 (over core), dates: 2 (over x).
Axes of the slice: x: 2, y: 2, z: 4, core: 2. Of those that a mesh axis runs over, the one named last changes fastest.
Arguments:
- imagery: bfloat16 [8, 4, 432, 4096], P(('groups', 'tiles'), 'cols', 'dates'), parts along dimension 0, may hold values from -6 to 6
- pixel_mask: int32 [8, 4, 4096], P(('groups', 'tiles'), ('cols', 'dates')), parts along dimension 0, may hold values 0 or 1
- point_pixel: int32 [8, 4, 4096], P(('groups', 'tiles'), ('cols', 'dates')), parts along dimension 0, may hold values from 0 to 4095
- point_yield: float32 [8, 4, 4096], P(('groups', 'tiles'), ('cols', 'dates')), parts along dimension 0, may hold values from -6 to 6
Outputs:
- prediction: float32 [8, 4, 4096], P(('groups', 'tiles'), ('cols', 'dates')), parts along dimension 0
- distance: float32 [8, 4, 4096], P(('groups', 'tiles'), ('cols', 'dates')), parts along dimension 0
- residual: float32 [8, 4, 4096], P(('groups', 'tiles'), ('cols', 'dates')), parts along dimension 0
The draws below stay inside these ranges and needn't reach their ends.
There are 2 independent parts, one for each index of `groups`. The reference program is written for one: setup_inputs(seed, part) draws one part's arguments, and reference() takes and returns one part's arrays. A program takes and returns all parts, laid end to end along the dimension named above; each array names one. Nothing has to cross between parts.
All inputs are finite; a program needn't handle non-finite values. No bound on the sum of `pixel_mask` on one device may be relied on, other than what follows from the above.
Results may differ from the reference program's by a relative error of at most 0.0003.
Values may be sent and summed in bfloat16 or wider, within the bound.
A program may use at most 128 MiB of HBM per device.

```python
import math
import jax
import jax.numpy as jnp
from jax import lax

F = 432
PIX = 4096
NPTS = 4096
GRID_ROWS = 4
GRID_COLS = 4


def draw_imagery(key, part):
    subkeys = jax.random.split(key, 5)
    full_shape = (GRID_ROWS, GRID_COLS, F, PIX)
    pixel_shape = (GRID_ROWS, GRID_COLS, 1, PIX)
    noise_scale = jnp.exp(jax.random.uniform(subkeys[0], (1, 1, F, 1), jnp.float32, math.log(0.1), 0.0))
    loading = jax.random.uniform(subkeys[1], (1, 1, F, 1), jnp.float32, -1.2, 1.2)
    tile_gain = jnp.exp(jax.random.uniform(subkeys[2], (GRID_ROWS, GRID_COLS, 1, 1), jnp.float32, math.log(0.7), math.log(1.4)))
    shared = jax.random.normal(subkeys[3], pixel_shape, jnp.float32)
    independent = jax.random.normal(subkeys[4], full_shape, jnp.float32)
    values = tile_gain * loading * shared + noise_scale * independent
    return jnp.clip(values, -6.0, 6.0).astype(jnp.bfloat16)


def with_ends(array, rng, smallest, top_value):
    place = [jax.random.randint(jax.random.fold_in(rng, axis), (), 0, length) for axis, length in enumerate(array.shape)]
    main_axis = array.shape.index(max(array.shape))
    neighbour = place[:main_axis] + [(place[main_axis] + 1) % array.shape[main_axis]] + place[main_axis + 1:]
    return array.at[tuple(place)].set(smallest).at[tuple(neighbour)].set(top_value)


def block_levels(key, dims, cuts, low, largest):
    def one(dim, parts):
        draws = jax.random.uniform(jax.random.fold_in(jax.random.fold_in(key, 6), dim), (parts,), jnp.float32, low / len(cuts), largest / len(cuts))
        return jnp.repeat(jnp.exp(draws), dims[dim] // parts).reshape((-1,) + (1,) * (len(dims) - dim - 1))

    loudness = one(*cuts[0])
    for cut in cuts[1:]:
        loudness = loudness * one(*cut)
    return loudness


def centred(rng, shape, scale, most, cuts=(), kind=jnp.bfloat16):
    loudness = block_levels(rng, shape, cuts, -0.22, 0.18) if cuts else 1.0
    entries = jax.random.normal(rng, shape, jnp.float32) * scale * loudness
    return jnp.minimum(jnp.maximum(entries, -most), most).astype(kind)


def setup_inputs(seed: int = 0, part: int = 0) -> dict:
    seeds = jax.random.split(jax.random.key(seed), 5)
    part_splits = jax.random.split(jax.random.fold_in(seeds[4], part), 5)
    return {
        "imagery": draw_imagery(jax.random.fold_in(jax.random.fold_in(seeds[4], part), 71), part),
        "pixel_mask": with_ends((jax.random.randint(part_splits[1], (GRID_ROWS, GRID_COLS, PIX), 0, 4) < 3).astype(jnp.int32), jax.random.fold_in(part_splits[1], 1), 0, 1),
        "point_pixel": with_ends(jax.random.randint(part_splits[2], (GRID_ROWS, GRID_COLS, NPTS), 0, PIX), jax.random.fold_in(part_splits[2], 1), 0, PIX - 1).astype(jnp.int32),
        "point_yield": centred(part_splits[3], (GRID_ROWS, GRID_COLS, NPTS), 1.0, 6.0, ((0, 4), (1, 4)), jnp.float32),
    }


ridge_term = 0.05

def lower_solve(factor, right):
    return lax.linalg.triangular_solve(factor, right, left_side=True, lower=True)

def chol_solve(factor, right):
    first = lower_solve(factor, right[:, None])
    second = lax.linalg.triangular_solve(factor, first, left_side=True, lower=True, transpose_a=True)
    return second[:, 0]

def tile_stats(args):
    feats, mask, index, yields = args
    feats32 = feats.astype(jnp.float32)
    counts = jax.ops.segment_sum(jnp.ones_like(index), index, num_segments=PIX)
    totals = jax.ops.segment_sum(yields, index, num_segments=PIX)
    weight = mask.astype(jnp.float32) * (counts > 0).astype(jnp.float32)
    target = totals / jnp.maximum(counts, 1).astype(jnp.float32)
    gram = jnp.dot(feats32 * weight[None, :], feats32.T, precision=lax.Precision.HIGHEST)
    moment = jnp.dot(feats32, weight * target, precision=lax.Precision.HIGHEST)
    return jnp.concatenate([gram, moment[None, :]], 0)

def tile_solve(args):
    feats, packed, index, yields = args
    feats32 = feats.astype(jnp.float32)
    system = packed[:F] / PIX + ridge_term * jnp.eye(F, dtype=jnp.float32)
    rhs = packed[F] / PIX
    factor = jnp.linalg.cholesky(system)
    beta = chol_solve(factor, rhs)
    fitted = jnp.dot(beta, feats32, precision=lax.Precision.HIGHEST)
    solved = lower_solve(factor, feats32)
    spread = jnp.sum(solved * solved, axis=0) / F
    return (fitted, spread, yields - fitted[index])

def reference(imagery, pixel_mask, point_pixel, point_yield):
    count = GRID_ROWS * GRID_COLS
    feats = imagery.reshape(count, F, PIX)
    masks = pixel_mask.reshape(count, PIX)
    index = point_pixel.reshape(count, NPTS)
    yields = point_yield.reshape(count, NPTS)
    packed = lax.map(tile_stats, (feats, masks, index, yields)).reshape(GRID_ROWS, GRID_COLS, F + 1, F)
    padded = jnp.pad(packed, ((1, 1), (1, 1), (0, 0), (0, 0)))
    kernel = (0.5, 1.0, 0.5)
    window = jnp.zeros_like(packed)
    for row in range(3):
        for col in range(3):
            window = window + kernel[row] * kernel[col] * padded[row:row + GRID_ROWS, col:col + GRID_COLS]
    fitted, spread, resid = lax.map(tile_solve, (feats, window.reshape(count, F + 1, F), index, yields))
    return (fitted.reshape(GRID_ROWS, GRID_COLS, PIX), spread.reshape(GRID_ROWS, GRID_COLS, PIX), resid.reshape(GRID_ROWS, GRID_COLS, NPTS))
```

```python
import jax
import jax.numpy as jnp
from jax import lax
from jax.experimental import pallas as pl
from jax.experimental.pallas import tpu as pltpu
from jax.sharding import PartitionSpec as P

ridge_term = 0.05
LANES = 128
CHUNK = 512
F32 = jnp.float32
BF16 = jnp.bfloat16
NT = (((1,), (1,)), ((), ()))


def split3(x):
    a = x.astype(BF16)
    rest = x - a.astype(F32)
    b = rest.astype(BF16)
    c = (rest - b.astype(F32)).astype(BF16)
    return a, b, c


def one_hots(index, rows):
    points = index.shape[1]
    high = lax.broadcasted_iota(jnp.int32, (rows, points), 0) == index // LANES
    low = lax.broadcasted_iota(jnp.int32, (LANES, points), 0) == index % LANES
    return high, low


def segment_kernel(index_ref, yield_ref, mask_ref, weight_ref, product_ref):
    rows = mask_ref.shape[0]
    high, low = one_hots(index_ref[...], rows)
    low = jnp.where(low, 1.0, 0.0).astype(BF16)
    pieces = [jnp.where(high, 1.0, 0.0).astype(BF16)]
    for piece in split3(yield_ref[...]):
        pieces.append(jnp.where(high, piece.astype(F32), 0.0).astype(BF16))
    sums = lax.dot_general(
        jnp.concatenate(pieces, 0), low, NT, preferred_element_type=F32
    )
    counts = sums[:rows]
    totals = sums[rows : 2 * rows] + sums[2 * rows : 3 * rows] + sums[3 * rows :]
    weight = jnp.where(counts > 0, mask_ref[...].astype(F32), 0.0)
    weight_ref[...] = weight
    product_ref[...] = weight * (totals / jnp.maximum(counts, 1.0))


def bands(width):
    blocks, offset = [], 0
    for i in range(pl.cdiv(width, LANES)):
        height = min(LANES, width - i * LANES)
        for j in range(i + 1):
            blocks.append((i, j, height, offset))
            offset += height
    return blocks, offset


def gram_kernel(feats_ref, weight_ref, product_ref, out_ref, acc):
    width, pixels = feats_ref.shape
    acc[...] = jnp.zeros_like(acc)

    def step(c, _):
        at = pl.multiple_of(c * CHUNK, CHUNK)
        feats = feats_ref[:, pl.ds(at, CHUNK)]
        left = []
        for s in range(CHUNK // LANES):
            row = pl.ds(c * (CHUNK // LANES) + s, 1)
            part = feats[:, s * LANES : (s + 1) * LANES]
            scaled = part * weight_ref[row, :].astype(BF16)
            a, b, d = (p.astype(F32) for p in split3(product_ref[row, :]))
            line = lax.broadcasted_iota(jnp.int32, (16, LANES), 0)
            extra = jnp.where(
                line == 0, a, jnp.where(line == 1, b, jnp.where(line == 2, d, 0.0))
            )
            left.append(jnp.concatenate([scaled, extra.astype(BF16)], 0))
        acc[...] += lax.dot_general(
            jnp.concatenate(left, 1), feats, NT, preferred_element_type=F32
        )
        return 0

    lax.fori_loop(0, pixels // CHUNK, step, 0)
    blocks, offset = bands(width)
    out_ref[...] = jnp.zeros_like(out_ref)
    for i, j, height, at in blocks:
        wide = min(LANES, width - j * LANES)
        out_ref[at : at + height, :wide] = acc[
            i * LANES : i * LANES + height, j * LANES : j * LANES + wide
        ]
    moment = acc[width : width + 1] + acc[width + 1 : width + 2]
    moment = moment + acc[width + 2 : width + 3]
    for j in range(pl.cdiv(width, LANES)):
        wide = min(LANES, width - j * LANES)
        out_ref[offset + j : offset + j + 1, :wide] = moment[
            :, j * LANES : j * LANES + wide
        ]


def small_inverse(p):
    n = len(p)
    for k in range(n):
        d = 1.0 / p[k][k]
        row = [d if j == k else p[k][j] * d for j in range(n)]
        new = []
        for i in range(n):
            if i == k:
                new.append(row)
            else:
                new.append(
                    [
                        -p[i][k] * d if j == k else p[i][j] - p[i][k] * row[j]
                        for j in range(n)
                    ]
                )
        p = new
    return p


def block_inverse(block, pivots, group=4):
    tiles = [block[8 * g : 8 * g + 8] for g in range(LANES // 8)]
    lane = lax.broadcasted_iota(jnp.int32, (8, LANES), 1)
    line = lax.broadcasted_iota(jnp.int32, (8, LANES), 0)
    for k in range(0, pivots, group):
        g, r = divmod(k, 8)
        cols = [
            [
                jnp.broadcast_to(t[:, k + j : k + j + 1], (8, LANES))
                for t in tiles
            ]
            for j in range(group)
        ]
        small = [
            [cols[j][g][r + i : r + i + 1] for j in range(group)]
            for i in range(group)
        ]
        small = small_inverse(small)
        rows = []
        for i in range(group):
            old = tiles[g][r + i : r + i + 1]
            old = jnp.where((lane[:1] >= k) & (lane[:1] < k + group), 0.0, old)
            rows.append(jnp.where(lane[:1] == k + i, 1.0, old))
        new_rows = []
        for i in range(group):
            total = small[i][0] * rows[0]
            for j in range(1, group):
                total = total + small[i][j] * rows[j]
            new_rows.append(jnp.broadcast_to(total, (8, LANES)))
        keep = (lane < k) | (lane >= k + group)
        for t in range(LANES // 8):
            value = jnp.where(keep, tiles[t], 0.0)
            for j in range(group):
                value = value - cols[j][t] * new_rows[j]
            if t == g:
                for i in range(group):
                    value = jnp.where(line == r + i, new_rows[i], value)
            tiles[t] = value
    return jnp.concatenate(tiles, 0)


def dot32(a, b):
    return jnp.dot(
        a, b, precision=lax.Precision.HIGHEST, preferred_element_type=F32
    )


def solve_kernel(
    packed_ref,
    feats_ref,
    index_ref,
    yield_ref,
    fitted_ref,
    spread_ref,
    resid_ref,
    system,
    base,
    high_ref,
    low_ref,
    fit,
):
    width, pixels = feats_ref.shape
    count = pl.cdiv(width, LANES)
    size = count * LANES
    blocks, offset = bands(width)
    scale = 1.0 / pixels
    line = lax.broadcasted_iota(jnp.int32, (LANES, LANES), 0)
    lane = lax.broadcasted_iota(jnp.int32, (LANES, LANES), 1)
    for i, j, height, at in blocks:
        value = packed_ref[at : at + height] * scale
        if height < LANES:
            value = jnp.concatenate(
                [value, jnp.zeros((LANES - height, LANES), F32)], 0
            )
        if i == j:
            diagonal = jnp.where(line < height, ridge_term, 1.0)
            value = value + jnp.where(line == lane, diagonal, 0.0)
        system[i * LANES : (i + 1) * LANES, j * LANES : (j + 1) * LANES] = value
        if i != j:
            system[j * LANES : (j + 1) * LANES, i * LANES : (i + 1) * LANES] = value.T

    base[...] = system[...]
    column = lax.broadcasted_iota(jnp.int32, (LANES, size), 1)
    wide_line = lax.broadcasted_iota(jnp.int32, (LANES, size), 0)

    def eliminate(k, pivots):
        at = k * LANES if isinstance(k, int) else pl.multiple_of(k * LANES, LANES)
        here = pl.ds(at, LANES)
        inverse = block_inverse(system[here, here], pivots)
        inside = (column >= at) & (column < at + LANES)
        unit = jnp.where(column == wide_line + at, 1.0, 0.0)
        right = dot32(inverse, jnp.where(inside, unit, system[here, :]))
        left = system[:, here]
        system[:, here] = jnp.zeros_like(left)
        system[...] -= dot32(left, right)
        system[here, :] = right

    full = width // LANES

    def body(k, _):
        eliminate(k, LANES)
        return 0

    lax.fori_loop(0, full, body, 0)
    if width % LANES:
        eliminate(full, width % LANES)

    rhs = jnp.concatenate(
        [packed_ref[offset + j : offset + j + 1] for j in range(count)], 1
    )
    rhs = jnp.broadcast_to(rhs * scale, (8, size))
    beta = dot32(rhs, system[...])
    beta = beta + dot32(rhs - dot32(beta, base[...]), system[...])
    beta = beta[:1, :width]
    inverse = system[:width, :width]
    upper = inverse.astype(BF16)
    a, b, d = (p.astype(F32) for p in split3(beta))
    row16 = lax.broadcasted_iota(jnp.int32, (16, width), 0)
    extra = jnp.where(row16 == 0, a, jnp.where(row16 == 1, b, jnp.where(row16 == 2, d, 0.0)))
    high_ref[...] = jnp.concatenate([upper, extra.astype(BF16)], 0)
    low_ref[...] = (inverse - upper.astype(F32)).astype(BF16)

    def step(c, _):
        at = pl.multiple_of(c * CHUNK, CHUNK)
        feats = feats_ref[:, pl.ds(at, CHUNK)]
        first = jnp.dot(high_ref[...], feats, preferred_element_type=F32)
        second = jnp.dot(low_ref[...], feats, preferred_element_type=F32)
        total = (first[:width] + second) * feats.astype(F32)
        spread_ref[:, pl.ds(at, CHUNK)] = jnp.sum(total, 0, keepdims=True) / width
        fitted = first[width : width + 1] + (
            first[width + 1 : width + 2] + first[width + 2 : width + 3]
        )
        fitted_ref[:, pl.ds(at, CHUNK)] = fitted
        for s in range(CHUNK // LANES):
            fit[pl.ds(c * (CHUNK // LANES) + s, 1), :] = fitted[
                :, s * LANES : (s + 1) * LANES
            ]
        return 0

    lax.fori_loop(0, pixels // CHUNK, step, 0)

    rows = pixels // LANES
    high, low = one_hots(index_ref[...], rows)
    low = jnp.where(low, 1.0, 0.0).astype(BF16)
    table = jnp.concatenate(split3(fit[...]), 0)
    found = jnp.dot(table, low, preferred_element_type=F32)
    found = found[:rows] + (found[rows : 2 * rows] + found[2 * rows :])
    value = jnp.sum(jnp.where(high, found, 0.0), 0, keepdims=True)
    resid_ref[...] = yield_ref[...] - value


PARAMS = pltpu.CompilerParams(vmem_limit_bytes=48 * 1024 * 1024)


def segments(index, yields, mask):
    shape = jax.ShapeDtypeStruct(mask.shape, F32)
    return pl.pallas_call(
        segment_kernel,
        out_shape=(shape, shape),
        compiler_params=PARAMS,
        cost_estimate=pl.CostEstimate(
            flops=2 * 128 * 128 * index.shape[1],
            bytes_accessed=16 * index.shape[1],
            transcendentals=0,
        ),
        name="segments",
    )(index, yields, mask)


def grams(feats, weight, product):
    width, pixels = feats.shape
    rows = bands(width)[1] + 8 * pl.cdiv(pl.cdiv(width, LANES), 8)
    return pl.pallas_call(
        gram_kernel,
        out_shape=jax.ShapeDtypeStruct((rows, LANES), F32),
        scratch_shapes=[pltpu.VMEM((width + 16, width), F32)],
        compiler_params=PARAMS,
        name="grams",
    )(feats, weight, product)


def solves(packed, feats, index, yields):
    width, pixels = feats.shape
    size = pl.cdiv(width, LANES) * LANES
    shape = jax.ShapeDtypeStruct((1, pixels), F32)
    return pl.pallas_call(
        solve_kernel,
        out_shape=(shape, shape, jax.ShapeDtypeStruct(yields.shape, F32)),
        scratch_shapes=[
            pltpu.VMEM((size, size), F32),
            pltpu.VMEM((size, size), F32),
            pltpu.VMEM((width + 16, width), BF16),
            pltpu.VMEM((width, width), BF16),
            pltpu.VMEM((pixels // LANES, LANES), F32),
        ],
        compiler_params=PARAMS,
        name="solves",
    )(packed, feats, index, yields)


def window(x, axis):
    devices = 1
    for name in axis if isinstance(axis, tuple) else (axis,):
        devices *= lax.axis_size(name)
    up = [(i, i + 1) for i in range(devices - 1)]
    down = [(j, i) for i, j in up]
    before = lax.ppermute(x, axis, up)
    after = lax.ppermute(x, axis, down)
    return 0.5 * before + x + 0.5 * after


def on_device(imagery, pixel_mask, point_pixel, point_yield):
    whole = lax.all_to_all(imagery, "dates", split_axis=1, concat_axis=2, tiled=True)
    feats = whole[0, 0]
    pixels = feats.shape[1]
    index = point_pixel[0]
    yields = point_yield[0]
    mask = pixel_mask.reshape(pixels // LANES, LANES)
    weight, product = segments(index, yields, mask)
    packed = grams(feats, weight, product)
    packed = window(packed, "tiles")
    packed = window(packed, ("cols", "dates"))
    fitted, spread, resid = solves(packed, feats, index, yields)
    return (fitted[None], spread[None], resid[None])


def solution(mesh):
    features = P(("groups", "tiles"), "cols", "dates", None)
    points = P(("groups", "tiles"), ("cols", "dates"), None)
    return jax.shard_map(
        on_device,
        mesh=mesh,
        in_specs=(features, points, points, points),
        out_specs=(points, points, points),
        check_vma=False,
    )
```

```python
import functools

import jax
import jax.numpy as jnp
from jax import lax
from jax.experimental import pallas as pl
from jax.experimental.pallas import tpu as pltpu
from jax.sharding import PartitionSpec as P

ridge_term = 0.05
LANES = 128
CHUNK = 512
PIECES = 4
F32 = jnp.float32
BF16 = jnp.bfloat16
NT = (((1,), (1,)), ((), ()))


def split3(x):
    a = x.astype(BF16)
    rest = x - a.astype(F32)
    b = rest.astype(BF16)
    c = (rest - b.astype(F32)).astype(BF16)
    return a, b, c


def one_hots(index, rows):
    points = index.shape[1]
    high = lax.broadcasted_iota(jnp.int32, (rows, points), 0) == index // LANES
    low = lax.broadcasted_iota(jnp.int32, (LANES, points), 0) == index % LANES
    return high, low


def segment_kernel(index_ref, yield_ref, mask_ref, weight_ref, product_ref):
    rows = mask_ref.shape[0]
    high, low = one_hots(index_ref[...], rows)
    low = jnp.where(low, 1.0, 0.0).astype(BF16)
    pieces = [jnp.where(high, 1.0, 0.0).astype(BF16)]
    for piece in split3(yield_ref[...]):
        pieces.append(jnp.where(high, piece.astype(F32), 0.0).astype(BF16))
    sums = lax.dot_general(
        jnp.concatenate(pieces, 0), low, NT, preferred_element_type=F32
    )
    counts = sums[:rows]
    totals = sums[rows : 2 * rows] + sums[2 * rows : 3 * rows] + sums[3 * rows :]
    weight = jnp.where(counts > 0, mask_ref[...].astype(F32), 0.0)
    weight_ref[...] = weight
    product_ref[...] = weight * (totals / jnp.maximum(counts, 1.0))


def bands(width):
    blocks, offset = [], 0
    for i in range(pl.cdiv(width, LANES)):
        height = min(LANES, width - i * LANES)
        for j in range(i + 1):
            blocks.append((i, j, height, offset))
            offset += height
    return blocks, offset


def gram_kernel(feats_ref, weight_ref, product_ref, out_ref, acc):
    width, pixels = feats_ref.shape
    acc[...] = jnp.zeros_like(acc)

    def step(c, _):
        at = pl.multiple_of(c * CHUNK, CHUNK)
        feats = feats_ref[:, pl.ds(at, CHUNK)]
        left = []
        for s in range(CHUNK // LANES):
            row = pl.ds(c * (CHUNK // LANES) + s, 1)
            part = feats[:, s * LANES : (s + 1) * LANES]
            scaled = part * weight_ref[row, :].astype(BF16)
            a, b, d = (p.astype(F32) for p in split3(product_ref[row, :]))
            line = lax.broadcasted_iota(jnp.int32, (16, LANES), 0)
            extra = jnp.where(
                line == 0, a, jnp.where(line == 1, b, jnp.where(line == 2, d, 0.0))
            )
            left.append(jnp.concatenate([scaled, extra.astype(BF16)], 0))
        acc[...] += lax.dot_general(
            jnp.concatenate(left, 1), feats, NT, preferred_element_type=F32
        )
        return 0

    lax.fori_loop(0, pixels // CHUNK, step, 0)
    blocks, offset = bands(width)
    out_ref[...] = jnp.zeros_like(out_ref)
    for i, j, height, at in blocks:
        wide = min(LANES, width - j * LANES)
        out_ref[at : at + height, :wide] = acc[
            i * LANES : i * LANES + height, j * LANES : j * LANES + wide
        ]
    moment = acc[width : width + 1] + acc[width + 1 : width + 2]
    moment = moment + acc[width + 2 : width + 3]
    for j in range(pl.cdiv(width, LANES)):
        wide = min(LANES, width - j * LANES)
        out_ref[offset + j : offset + j + 1, :wide] = moment[
            :, j * LANES : j * LANES + wide
        ]


def small_inverse(p):
    n = len(p)
    for k in range(n):
        d = 1.0 / p[k][k]
        row = [d if j == k else p[k][j] * d for j in range(n)]
        new = []
        for i in range(n):
            if i == k:
                new.append(row)
            else:
                new.append(
                    [
                        -p[i][k] * d if j == k else p[i][j] - p[i][k] * row[j]
                        for j in range(n)
                    ]
                )
        p = new
    return p


def block_inverse(block, pivots, group=4):
    tiles = [block[8 * g : 8 * g + 8] for g in range(LANES // 8)]
    lane = lax.broadcasted_iota(jnp.int32, (8, LANES), 1)
    line = lax.broadcasted_iota(jnp.int32, (8, LANES), 0)
    for k in range(0, pivots, group):
        g, r = divmod(k, 8)
        cols = [
            [
                jnp.broadcast_to(t[:, k + j : k + j + 1], (8, LANES))
                for t in tiles
            ]
            for j in range(group)
        ]
        small = [
            [cols[j][g][r + i : r + i + 1] for j in range(group)]
            for i in range(group)
        ]
        small = small_inverse(small)
        rows = []
        for i in range(group):
            old = tiles[g][r + i : r + i + 1]
            old = jnp.where((lane[:1] >= k) & (lane[:1] < k + group), 0.0, old)
            rows.append(jnp.where(lane[:1] == k + i, 1.0, old))
        new_rows = []
        for i in range(group):
            total = small[i][0] * rows[0]
            for j in range(1, group):
                total = total + small[i][j] * rows[j]
            new_rows.append(jnp.broadcast_to(total, (8, LANES)))
        keep = (lane < k) | (lane >= k + group)
        for t in range(LANES // 8):
            value = jnp.where(keep, tiles[t], 0.0)
            for j in range(group):
                value = value - cols[j][t] * new_rows[j]
            if t == g:
                for i in range(group):
                    value = jnp.where(line == r + i, new_rows[i], value)
            tiles[t] = value
    return jnp.concatenate(tiles, 0)


def dot32(a, b):
    return jnp.dot(
        a, b, precision=lax.Precision.HIGHEST, preferred_element_type=F32
    )


def solve_kernel(
    packed_ref,
    feats_ref,
    index_ref,
    yield_ref,
    fitted_ref,
    spread_ref,
    resid_ref,
    system,
    base,
    high_ref,
    low_ref,
    fit,
):
    width, pixels = feats_ref.shape
    count = pl.cdiv(width, LANES)
    size = count * LANES
    blocks, offset = bands(width)
    scale = 1.0 / pixels
    line = lax.broadcasted_iota(jnp.int32, (LANES, LANES), 0)
    lane = lax.broadcasted_iota(jnp.int32, (LANES, LANES), 1)
    for i, j, height, at in blocks:
        value = packed_ref[at : at + height] * scale
        if height < LANES:
            value = jnp.concatenate(
                [value, jnp.zeros((LANES - height, LANES), F32)], 0
            )
        if i == j:
            diagonal = jnp.where(line < height, ridge_term, 1.0)
            value = value + jnp.where(line == lane, diagonal, 0.0)
        system[i * LANES : (i + 1) * LANES, j * LANES : (j + 1) * LANES] = value
        if i != j:
            system[j * LANES : (j + 1) * LANES, i * LANES : (i + 1) * LANES] = value.T

    base[...] = system[...]
    column = lax.broadcasted_iota(jnp.int32, (LANES, size), 1)
    wide_line = lax.broadcasted_iota(jnp.int32, (LANES, size), 0)

    def eliminate(k, pivots):
        at = k * LANES if isinstance(k, int) else pl.multiple_of(k * LANES, LANES)
        here = pl.ds(at, LANES)
        inverse = block_inverse(system[here, here], pivots)
        inside = (column >= at) & (column < at + LANES)
        unit = jnp.where(column == wide_line + at, 1.0, 0.0)
        right = dot32(inverse, jnp.where(inside, unit, system[here, :]))
        left = system[:, here]
        system[:, here] = jnp.zeros_like(left)
        system[...] -= dot32(left, right)
        system[here, :] = right

    full = width // LANES

    def body(k, _):
        eliminate(k, LANES)
        return 0

    lax.fori_loop(0, full, body, 0)
    if width % LANES:
        eliminate(full, width % LANES)

    rhs = jnp.concatenate(
        [packed_ref[offset + j : offset + j + 1] for j in range(count)], 1
    )
    rhs = jnp.broadcast_to(rhs * scale, (8, size))
    beta = dot32(rhs, system[...])
    beta = beta + dot32(rhs - dot32(beta, base[...]), system[...])
    beta = beta[:1, :width]
    inverse = system[:width, :width]
    upper = inverse.astype(BF16)
    a, b, d = (p.astype(F32) for p in split3(beta))
    row16 = lax.broadcasted_iota(jnp.int32, (16, width), 0)
    extra = jnp.where(row16 == 0, a, jnp.where(row16 == 1, b, jnp.where(row16 == 2, d, 0.0)))
    high_ref[...] = jnp.concatenate([upper, extra.astype(BF16)], 0)
    low_ref[...] = (inverse - upper.astype(F32)).astype(BF16)

    def step(c, _):
        at = pl.multiple_of(c * CHUNK, CHUNK)
        feats = feats_ref[:, pl.ds(at, CHUNK)]
        first = jnp.dot(high_ref[...], feats, preferred_element_type=F32)
        second = jnp.dot(low_ref[...], feats, preferred_element_type=F32)
        total = (first[:width] + second) * feats.astype(F32)
        spread_ref[:, pl.ds(at, CHUNK)] = jnp.sum(total, 0, keepdims=True) / width
        fitted = first[width : width + 1] + (
            first[width + 1 : width + 2] + first[width + 2 : width + 3]
        )
        fitted_ref[:, pl.ds(at, CHUNK)] = fitted
        for s in range(CHUNK // LANES):
            fit[pl.ds(c * (CHUNK // LANES) + s, 1), :] = fitted[
                :, s * LANES : (s + 1) * LANES
            ]
        return 0

    lax.fori_loop(0, pixels // CHUNK, step, 0)

    rows = pixels // LANES
    high, low = one_hots(index_ref[...], rows)
    low = jnp.where(low, 1.0, 0.0).astype(BF16)
    table = jnp.concatenate(split3(fit[...]), 0)
    found = jnp.dot(table, low, preferred_element_type=F32)
    found = found[:rows] + (found[rows : 2 * rows] + found[2 * rows :])
    value = jnp.sum(jnp.where(high, found, 0.0), 0, keepdims=True)
    resid_ref[...] = yield_ref[...] - value


PARAMS = pltpu.CompilerParams(vmem_limit_bytes=48 * 1024 * 1024)


def segments(index, yields, mask):
    shape = jax.ShapeDtypeStruct(mask.shape, F32)
    return pl.pallas_call(
        segment_kernel,
        out_shape=(shape, shape),
        compiler_params=PARAMS,
        cost_estimate=pl.CostEstimate(
            flops=2 * 128 * 128 * index.shape[1],
            bytes_accessed=16 * index.shape[1],
            transcendentals=0,
        ),
        name="segments",
    )(index, yields, mask)


def grams(feats, weight, product):
    width, pixels = feats.shape
    rows = bands(width)[1] + 8 * pl.cdiv(pl.cdiv(width, LANES), 8)
    return pl.pallas_call(
        gram_kernel,
        out_shape=jax.ShapeDtypeStruct((rows, LANES), F32),
        scratch_shapes=[pltpu.VMEM((width + 16, width), F32)],
        compiler_params=PARAMS,
        name="grams",
    )(feats, weight, product)


def solves(packed, feats, index, yields):
    width, pixels = feats.shape
    size = pl.cdiv(width, LANES) * LANES
    shape = jax.ShapeDtypeStruct((1, pixels), F32)
    return pl.pallas_call(
        solve_kernel,
        out_shape=(shape, shape, jax.ShapeDtypeStruct(yields.shape, F32)),
        scratch_shapes=[
            pltpu.VMEM((size, size), F32),
            pltpu.VMEM((size, size), F32),
            pltpu.VMEM((width + 16, width), BF16),
            pltpu.VMEM((width, width), BF16),
            pltpu.VMEM((pixels // LANES, LANES), F32),
        ],
        compiler_params=PARAMS,
        name="solves",
    )(packed, feats, index, yields)


def window_kernel(shape, own_ref, out_ref, landed, middle, send_sem, recv_sem):
    tiles, cols, dates = shape
    row = lax.axis_index("tiles")
    col = lax.axis_index("cols") * dates + lax.axis_index("dates")
    total = own_ref.shape[0]
    step = -(-total // (8 * PIECES)) * 8
    pieces = [pl.ds(at, min(step, total - at)) for at in range(0, total, step)]

    def place(c):
        return {"cols": c // dates, "dates": c % dates}

    links = (
        (row < tiles - 1, lambda: {"tiles": row + 1}, row > 0, lambda: {"tiles": row - 1}),
        (row > 0, lambda: {"tiles": row - 1}, row < tiles - 1, lambda: {"tiles": row + 1}),
        (col < cols * dates - 1, lambda: place(col + 1), col > 0, lambda: place(col - 1)),
        (col > 0, lambda: place(col - 1), col < cols * dates - 1, lambda: place(col + 1)),
    )

    def copy(d, i, source, device):
        return pltpu.make_async_remote_copy(
            src_ref=source.at[pieces[i]],
            dst_ref=landed.at[d, pieces[i]],
            send_sem=send_sem.at[d, i],
            recv_sem=recv_sem.at[d, i],
            device_id=device,
            device_id_type=pl.DeviceIdType.MESH,
        )

    barrier = pltpu.get_barrier_semaphore()
    for there, target, _, _ in links:

        @pl.when(there)
        def _(target=target):
            pl.semaphore_signal(
                barrier, inc=1, device_id=target(), device_id_type=pl.DeviceIdType.MESH
            )

    peers = sum(there.astype(jnp.int32) for there, _, _, _ in links)
    pl.semaphore_wait(barrier, peers)

    def send(d, i, source):
        there, target, _, _ = links[d]

        @pl.when(there)
        def _():
            copy(d, i, source, target()).start()

    def receive(d, i, source, into):
        _, _, there, origin = links[d]

        @pl.when(there)
        def _():
            copy(d, i, source, origin()).wait_recv()
            into[pieces[i]] += 0.5 * landed[d, pieces[i]]

    count = len(pieces)
    for i in range(count):
        send(0, i, own_ref)
        send(1, i, own_ref)
    for i in range(count):
        middle[pieces[i]] = own_ref[pieces[i]]
        receive(0, i, own_ref, middle)
        receive(1, i, own_ref, middle)
        send(2, i, middle)
        send(3, i, middle)
    for i in range(count):
        out_ref[pieces[i]] = middle[pieces[i]]
        receive(2, i, middle, out_ref)
        receive(3, i, middle, out_ref)
    for i in range(count):
        for d in range(4):
            there, target, _, _ = links[d]

            @pl.when(there)
            def _(d=d, i=i, target=target):
                copy(d, i, own_ref if d < 2 else middle, target()).wait_send()


def window(packed):
    shape = tuple(lax.axis_size(name) for name in ("tiles", "cols", "dates"))
    in_vmem = pl.BlockSpec(memory_space=pltpu.VMEM)
    return pl.pallas_call(
        functools.partial(window_kernel, shape),
        out_shape=jax.ShapeDtypeStruct(packed.shape, F32),
        in_specs=[in_vmem],
        out_specs=in_vmem,
        scratch_shapes=[
            pltpu.VMEM((4,) + packed.shape, F32),
            pltpu.VMEM(packed.shape, F32),
            pltpu.SemaphoreType.DMA((4, PIECES)),
            pltpu.SemaphoreType.DMA((4, PIECES)),
        ],
        compiler_params=pltpu.CompilerParams(
            collective_id=0,
            has_side_effects=True,
            vmem_limit_bytes=48 * 1024 * 1024,
        ),
        name="window",
    )(packed)


def on_device(imagery, pixel_mask, point_pixel, point_yield):
    whole = lax.all_to_all(imagery, "dates", split_axis=1, concat_axis=2, tiled=True)
    feats = whole[0, 0]
    pixels = feats.shape[1]
    index = point_pixel[0]
    yields = point_yield[0]
    mask = pixel_mask.reshape(pixels // LANES, LANES)
    weight, product = segments(index, yields, mask)
    packed = grams(feats, weight, product)
    packed = window(packed)
    fitted, spread, resid = solves(packed, feats, index, yields)
    return (fitted[None], spread[None], resid[None])


def solution(mesh):
    features = P(("groups", "tiles"), "cols", "dates", None)
    points = P(("groups", "tiles"), ("cols", "dates"), None)
    return jax.shard_map(
        on_device,
        mesh=mesh,
        in_specs=(features, points, points, points),
        out_specs=(points, points, points),
        check_vma=False,
    )
```

```python
import functools

import jax
import jax.numpy as jnp
from jax import lax
from jax.experimental import pallas as pl
from jax.experimental.pallas import tpu as pltpu
from jax.sharding import PartitionSpec as P

ridge_term = 0.05
LANES = 128
CHUNK = 512
PIECES = 8
F32 = jnp.float32
BF16 = jnp.bfloat16
NT = (((1,), (1,)), ((), ()))


def split3(x):
    a = x.astype(BF16)
    rest = x - a.astype(F32)
    b = rest.astype(BF16)
    c = (rest - b.astype(F32)).astype(BF16)
    return a, b, c


def one_hots(index, rows):
    points = index.shape[1]
    high = lax.broadcasted_iota(jnp.int32, (rows, points), 0) == index // LANES
    low = lax.broadcasted_iota(jnp.int32, (LANES, points), 0) == index % LANES
    return high, low


def segment_kernel(index_ref, yield_ref, mask_ref, weight_ref, product_ref):
    rows = mask_ref.shape[0]
    high, low = one_hots(index_ref[...], rows)
    low = jnp.where(low, 1.0, 0.0).astype(BF16)
    pieces = [jnp.where(high, 1.0, 0.0).astype(BF16)]
    for piece in split3(yield_ref[...]):
        pieces.append(jnp.where(high, piece.astype(F32), 0.0).astype(BF16))
    sums = lax.dot_general(
        jnp.concatenate(pieces, 0), low, NT, preferred_element_type=F32
    )
    counts = sums[:rows]
    totals = sums[rows : 2 * rows] + sums[2 * rows : 3 * rows] + sums[3 * rows :]
    weight = jnp.where(counts > 0, mask_ref[...].astype(F32), 0.0)
    weight_ref[...] = weight
    product_ref[...] = weight * (totals / jnp.maximum(counts, 1.0))


def bands(width):
    blocks, offset = [], 0
    for i in range(pl.cdiv(width, LANES)):
        height = min(LANES, width - i * LANES)
        for j in range(i + 1):
            blocks.append((i, j, height, offset))
            offset += height
    return blocks, offset


def gram_kernel(feats_ref, weight_ref, product_ref, out_ref, acc):
    width, pixels = feats_ref.shape
    acc[...] = jnp.zeros_like(acc)

    def step(c, _):
        at = pl.multiple_of(c * CHUNK, CHUNK)
        feats = feats_ref[:, pl.ds(at, CHUNK)]
        left = []
        for s in range(CHUNK // LANES):
            row = pl.ds(c * (CHUNK // LANES) + s, 1)
            part = feats[:, s * LANES : (s + 1) * LANES]
            scaled = part * weight_ref[row, :].astype(BF16)
            a, b, d = (p.astype(F32) for p in split3(product_ref[row, :]))
            line = lax.broadcasted_iota(jnp.int32, (16, LANES), 0)
            extra = jnp.where(
                line == 0, a, jnp.where(line == 1, b, jnp.where(line == 2, d, 0.0))
            )
            left.append(jnp.concatenate([scaled, extra.astype(BF16)], 0))
        acc[...] += lax.dot_general(
            jnp.concatenate(left, 1), feats, NT, preferred_element_type=F32
        )
        return 0

    lax.fori_loop(0, pixels // CHUNK, step, 0)
    blocks, offset = bands(width)
    out_ref[...] = jnp.zeros_like(out_ref)
    for i, j, height, at in blocks:
        wide = min(LANES, width - j * LANES)
        out_ref[at : at + height, :wide] = acc[
            i * LANES : i * LANES + height, j * LANES : j * LANES + wide
        ]
    moment = acc[width : width + 1] + acc[width + 1 : width + 2]
    moment = moment + acc[width + 2 : width + 3]
    for j in range(pl.cdiv(width, LANES)):
        wide = min(LANES, width - j * LANES)
        out_ref[offset + j : offset + j + 1, :wide] = moment[
            :, j * LANES : j * LANES + wide
        ]


def small_inverse(p):
    n = len(p)
    for k in range(n):
        d = 1.0 / p[k][k]
        row = [d if j == k else p[k][j] * d for j in range(n)]
        new = []
        for i in range(n):
            if i == k:
                new.append(row)
            else:
                new.append(
                    [
                        -p[i][k] * d if j == k else p[i][j] - p[i][k] * row[j]
                        for j in range(n)
                    ]
                )
        p = new
    return p


def block_inverse(block, pivots, group=4):
    tiles = [block[8 * g : 8 * g + 8] for g in range(LANES // 8)]
    lane = lax.broadcasted_iota(jnp.int32, (8, LANES), 1)
    line = lax.broadcasted_iota(jnp.int32, (8, LANES), 0)
    for k in range(0, pivots, group):
        g, r = divmod(k, 8)
        cols = [
            [
                jnp.broadcast_to(t[:, k + j : k + j + 1], (8, LANES))
                for t in tiles
            ]
            for j in range(group)
        ]
        small = [
            [cols[j][g][r + i : r + i + 1] for j in range(group)]
            for i in range(group)
        ]
        small = small_inverse(small)
        rows = []
        for i in range(group):
            old = tiles[g][r + i : r + i + 1]
            old = jnp.where((lane[:1] >= k) & (lane[:1] < k + group), 0.0, old)
            rows.append(jnp.where(lane[:1] == k + i, 1.0, old))
        new_rows = []
        for i in range(group):
            total = small[i][0] * rows[0]
            for j in range(1, group):
                total = total + small[i][j] * rows[j]
            new_rows.append(jnp.broadcast_to(total, (8, LANES)))
        keep = (lane < k) | (lane >= k + group)
        for t in range(LANES // 8):
            value = jnp.where(keep, tiles[t], 0.0)
            for j in range(group):
                value = value - cols[j][t] * new_rows[j]
            if t == g:
                for i in range(group):
                    value = jnp.where(line == r + i, new_rows[i], value)
            tiles[t] = value
    return jnp.concatenate(tiles, 0)


def dot32(a, b):
    return jnp.dot(
        a, b, precision=lax.Precision.HIGHEST, preferred_element_type=F32
    )


def solve_kernel(
    packed_ref,
    feats_ref,
    index_ref,
    yield_ref,
    fitted_ref,
    spread_ref,
    resid_ref,
    system,
    base,
    high_ref,
    low_ref,
    fit,
):
    width, pixels = feats_ref.shape
    count = pl.cdiv(width, LANES)
    size = count * LANES
    blocks, offset = bands(width)
    scale = 1.0 / pixels
    line = lax.broadcasted_iota(jnp.int32, (LANES, LANES), 0)
    lane = lax.broadcasted_iota(jnp.int32, (LANES, LANES), 1)
    for i, j, height, at in blocks:
        value = packed_ref[at : at + height] * scale
        if height < LANES:
            value = jnp.concatenate(
                [value, jnp.zeros((LANES - height, LANES), F32)], 0
            )
        if i == j:
            diagonal = jnp.where(line < height, ridge_term, 1.0)
            value = value + jnp.where(line == lane, diagonal, 0.0)
        system[i * LANES : (i + 1) * LANES, j * LANES : (j + 1) * LANES] = value
        if i != j:
            system[j * LANES : (j + 1) * LANES, i * LANES : (i + 1) * LANES] = value.T

    base[...] = system[...]
    column = lax.broadcasted_iota(jnp.int32, (LANES, size), 1)
    wide_line = lax.broadcasted_iota(jnp.int32, (LANES, size), 0)

    def eliminate(k, pivots):
        at = k * LANES if isinstance(k, int) else pl.multiple_of(k * LANES, LANES)
        here = pl.ds(at, LANES)
        inverse = block_inverse(system[here, here], pivots)
        inside = (column >= at) & (column < at + LANES)
        unit = jnp.where(column == wide_line + at, 1.0, 0.0)
        right = dot32(inverse, jnp.where(inside, unit, system[here, :]))
        left = system[:, here]
        system[:, here] = jnp.zeros_like(left)
        system[...] -= dot32(left, right)
        system[here, :] = right

    full = width // LANES

    def body(k, _):
        eliminate(k, LANES)
        return 0

    lax.fori_loop(0, full, body, 0)
    if width % LANES:
        eliminate(full, width % LANES)

    rhs = jnp.concatenate(
        [packed_ref[offset + j : offset + j + 1] for j in range(count)], 1
    )
    rhs = jnp.broadcast_to(rhs * scale, (8, size))
    beta = dot32(rhs, system[...])
    beta = beta + dot32(rhs - dot32(beta, base[...]), system[...])
    beta = beta[:1, :width]
    inverse = system[:width, :width]
    upper = inverse.astype(BF16)
    a, b, d = (p.astype(F32) for p in split3(beta))
    row16 = lax.broadcasted_iota(jnp.int32, (16, width), 0)
    extra = jnp.where(row16 == 0, a, jnp.where(row16 == 1, b, jnp.where(row16 == 2, d, 0.0)))
    high_ref[...] = jnp.concatenate([upper, extra.astype(BF16)], 0)
    low_ref[...] = (inverse - upper.astype(F32)).astype(BF16)

    def step(c, _):
        at = pl.multiple_of(c * CHUNK, CHUNK)
        feats = feats_ref[:, pl.ds(at, CHUNK)]
        first = jnp.dot(high_ref[...], feats, preferred_element_type=F32)
        second = jnp.dot(low_ref[...], feats, preferred_element_type=F32)
        total = (first[:width] + second) * feats.astype(F32)
        spread_ref[:, pl.ds(at, CHUNK)] = jnp.sum(total, 0, keepdims=True) / width
        fitted = first[width : width + 1] + (
            first[width + 1 : width + 2] + first[width + 2 : width + 3]
        )
        fitted_ref[:, pl.ds(at, CHUNK)] = fitted
        for s in range(CHUNK // LANES):
            fit[pl.ds(c * (CHUNK // LANES) + s, 1), :] = fitted[
                :, s * LANES : (s + 1) * LANES
            ]
        return 0

    lax.fori_loop(0, pixels // CHUNK, step, 0)

    rows = pixels // LANES
    high, low = one_hots(index_ref[...], rows)
    low = jnp.where(low, 1.0, 0.0).astype(BF16)
    table = jnp.concatenate(split3(fit[...]), 0)
    found = jnp.dot(table, low, preferred_element_type=F32)
    found = found[:rows] + (found[rows : 2 * rows] + found[2 * rows :])
    value = jnp.sum(jnp.where(high, found, 0.0), 0, keepdims=True)
    resid_ref[...] = yield_ref[...] - value


PARAMS = pltpu.CompilerParams(vmem_limit_bytes=48 * 1024 * 1024)


def segments(index, yields, mask):
    shape = jax.ShapeDtypeStruct(mask.shape, F32)
    return pl.pallas_call(
        segment_kernel,
        out_shape=(shape, shape),
        compiler_params=PARAMS,
        cost_estimate=pl.CostEstimate(
            flops=2 * 128 * 128 * index.shape[1],
            bytes_accessed=16 * index.shape[1],
            transcendentals=0,
        ),
        name="segments",
    )(index, yields, mask)


def grams(feats, weight, product):
    width, pixels = feats.shape
    rows = bands(width)[1] + 8 * pl.cdiv(pl.cdiv(width, LANES), 8)
    return pl.pallas_call(
        gram_kernel,
        out_shape=jax.ShapeDtypeStruct((rows, LANES), F32),
        scratch_shapes=[pltpu.VMEM((width + 16, width), F32)],
        compiler_params=PARAMS,
        name="grams",
    )(feats, weight, product)


def solves(packed, feats, index, yields):
    width, pixels = feats.shape
    size = pl.cdiv(width, LANES) * LANES
    shape = jax.ShapeDtypeStruct((1, pixels), F32)
    return pl.pallas_call(
        solve_kernel,
        out_shape=(shape, shape, jax.ShapeDtypeStruct(yields.shape, F32)),
        scratch_shapes=[
            pltpu.VMEM((size, size), F32),
            pltpu.VMEM((size, size), F32),
            pltpu.VMEM((width + 16, width), BF16),
            pltpu.VMEM((width, width), BF16),
            pltpu.VMEM((pixels // LANES, LANES), F32),
        ],
        compiler_params=PARAMS,
        name="solves",
    )(packed, feats, index, yields)


def window_kernel(shape, own_ref, out_ref, landed, middle, send_sem, recv_sem):
    tiles, cols, dates = shape
    row = lax.axis_index("tiles")
    col = lax.axis_index("cols") * dates + lax.axis_index("dates")
    total = own_ref.shape[0]
    step = -(-total // (8 * PIECES)) * 8
    pieces = [pl.ds(at, min(step, total - at)) for at in range(0, total, step)]

    def place(c):
        return {"cols": c // dates, "dates": c % dates}

    links = (
        (row < tiles - 1, lambda: {"tiles": row + 1}, row > 0, lambda: {"tiles": row - 1}),
        (row > 0, lambda: {"tiles": row - 1}, row < tiles - 1, lambda: {"tiles": row + 1}),
        (col < cols * dates - 1, lambda: place(col + 1), col > 0, lambda: place(col - 1)),
        (col > 0, lambda: place(col - 1), col < cols * dates - 1, lambda: place(col + 1)),
    )

    def copy(d, i, source, device):
        return pltpu.make_async_remote_copy(
            src_ref=source.at[pieces[i]],
            dst_ref=landed.at[d, pieces[i]],
            send_sem=send_sem.at[d, i],
            recv_sem=recv_sem.at[d, i],
            device_id=device,
            device_id_type=pl.DeviceIdType.MESH,
        )

    barrier = pltpu.get_barrier_semaphore()
    for there, target, _, _ in links:

        @pl.when(there)
        def _(target=target):
            pl.semaphore_signal(
                barrier, inc=1, device_id=target(), device_id_type=pl.DeviceIdType.MESH
            )

    peers = sum(there.astype(jnp.int32) for there, _, _, _ in links)
    pl.semaphore_wait(barrier, peers)

    def send(d, i, source):
        there, target, _, _ = links[d]

        @pl.when(there)
        def _():
            copy(d, i, source, target()).start()

    def receive(d, i, source, into):
        _, _, there, origin = links[d]

        @pl.when(there)
        def _():
            copy(d, i, source, origin()).wait_recv()
            into[pieces[i]] += 0.5 * landed[d, pieces[i]]

    count = len(pieces)
    for i in range(count):
        send(0, i, own_ref)
        send(1, i, own_ref)
    for i in range(count):
        middle[pieces[i]] = own_ref[pieces[i]]
        receive(0, i, own_ref, middle)
        receive(1, i, own_ref, middle)
        send(2, i, middle)
        send(3, i, middle)
    for i in range(count):
        out_ref[pieces[i]] = middle[pieces[i]]
        receive(2, i, middle, out_ref)
        receive(3, i, middle, out_ref)
    for i in range(count):
        for d in range(4):
            there, target, _, _ = links[d]

            @pl.when(there)
            def _(d=d, i=i, target=target):
                copy(d, i, own_ref if d < 2 else middle, target()).wait_send()


def window(packed):
    shape = tuple(lax.axis_size(name) for name in ("tiles", "cols", "dates"))
    in_vmem = pl.BlockSpec(memory_space=pltpu.VMEM)
    return pl.pallas_call(
        functools.partial(window_kernel, shape),
        out_shape=jax.ShapeDtypeStruct(packed.shape, F32),
        in_specs=[in_vmem],
        out_specs=in_vmem,
        scratch_shapes=[
            pltpu.VMEM((4,) + packed.shape, F32),
            pltpu.VMEM(packed.shape, F32),
            pltpu.SemaphoreType.DMA((4, PIECES)),
            pltpu.SemaphoreType.DMA((4, PIECES)),
        ],
        compiler_params=pltpu.CompilerParams(
            collective_id=0,
            has_side_effects=True,
            vmem_limit_bytes=48 * 1024 * 1024,
        ),
        name="window",
    )(packed)


def on_device(imagery, pixel_mask, point_pixel, point_yield):
    whole = lax.all_to_all(imagery, "dates", split_axis=1, concat_axis=2, tiled=True)
    feats = whole[0, 0]
    pixels = feats.shape[1]
    index = point_pixel[0]
    yields = point_yield[0]
    mask = pixel_mask.reshape(pixels // LANES, LANES)
    weight, product = segments(index, yields, mask)
    packed = grams(feats, weight, product)
    packed = window(packed)
    fitted, spread, resid = solves(packed, feats, index, yields)
    return (fitted[None], spread[None], resid[None])


def solution(mesh):
    features = P(("groups", "tiles"), "cols", "dates", None)
    points = P(("groups", "tiles"), ("cols", "dates"), None)
    return jax.shard_map(
        on_device,
        mesh=mesh,
        in_specs=(features, points, points, points),
        out_specs=(points, points, points),
        check_vma=False,
    )
```

```python
import functools

import jax
import jax.numpy as jnp
from jax import lax
from jax.experimental import pallas as pl
from jax.experimental.pallas import tpu as pltpu
from jax.sharding import PartitionSpec as P

ridge_term = 0.05
LANES = 128
CHUNK = 512
PIECES = 8
F32 = jnp.float32
BF16 = jnp.bfloat16
NT = (((1,), (1,)), ((), ()))


def split3(x):
    a = x.astype(BF16)
    rest = x - a.astype(F32)
    b = rest.astype(BF16)
    c = (rest - b.astype(F32)).astype(BF16)
    return a, b, c


def one_hots(index, rows):
    points = index.shape[1]
    high = lax.broadcasted_iota(jnp.int32, (rows, points), 0) == index // LANES
    low = lax.broadcasted_iota(jnp.int32, (LANES, points), 0) == index % LANES
    return high, low


def segment_kernel(index_ref, yield_ref, mask_ref, weight_ref, product_ref):
    rows = mask_ref.shape[0]
    high, low = one_hots(index_ref[...], rows)
    low = jnp.where(low, 1.0, 0.0).astype(BF16)
    pieces = [jnp.where(high, 1.0, 0.0).astype(BF16)]
    for piece in split3(yield_ref[...]):
        pieces.append(jnp.where(high, piece.astype(F32), 0.0).astype(BF16))
    sums = lax.dot_general(
        jnp.concatenate(pieces, 0), low, NT, preferred_element_type=F32
    )
    counts = sums[:rows]
    totals = sums[rows : 2 * rows] + sums[2 * rows : 3 * rows] + sums[3 * rows :]
    weight = jnp.where(counts > 0, mask_ref[...].astype(F32), 0.0)
    weight_ref[...] = weight
    product_ref[...] = weight * (totals / jnp.maximum(counts, 1.0))


def bands(width):
    blocks, offset = [], 0
    for i in range(pl.cdiv(width, LANES)):
        height = min(LANES, width - i * LANES)
        for j in range(i + 1):
            blocks.append((i, j, height, offset))
            offset += height
    return blocks, offset


def gram_kernel(feats_ref, weight_ref, product_ref, out_ref, acc):
    width, pixels = feats_ref.shape
    acc[...] = jnp.zeros_like(acc)

    def step(c, _):
        at = pl.multiple_of(c * CHUNK, CHUNK)
        feats = feats_ref[:, pl.ds(at, CHUNK)]
        left = []
        for s in range(CHUNK // LANES):
            row = pl.ds(c * (CHUNK // LANES) + s, 1)
            part = feats[:, s * LANES : (s + 1) * LANES]
            scaled = part * weight_ref[row, :].astype(BF16)
            a, b, d = (p.astype(F32) for p in split3(product_ref[row, :]))
            line = lax.broadcasted_iota(jnp.int32, (16, LANES), 0)
            extra = jnp.where(
                line == 0, a, jnp.where(line == 1, b, jnp.where(line == 2, d, 0.0))
            )
            left.append(jnp.concatenate([scaled, extra.astype(BF16)], 0))
        acc[...] += lax.dot_general(
            jnp.concatenate(left, 1), feats, NT, preferred_element_type=F32
        )
        return 0

    lax.fori_loop(0, pixels // CHUNK, step, 0)
    blocks, offset = bands(width)
    out_ref[...] = jnp.zeros_like(out_ref)
    for i, j, height, at in blocks:
        wide = min(LANES, width - j * LANES)
        out_ref[at : at + height, :wide] = acc[
            i * LANES : i * LANES + height, j * LANES : j * LANES + wide
        ]
    moment = acc[width : width + 1] + acc[width + 1 : width + 2]
    moment = moment + acc[width + 2 : width + 3]
    for j in range(pl.cdiv(width, LANES)):
        wide = min(LANES, width - j * LANES)
        out_ref[offset + j : offset + j + 1, :wide] = moment[
            :, j * LANES : j * LANES + wide
        ]


def small_inverse(p):
    n = len(p)
    for k in range(n):
        d = 1.0 / p[k][k]
        row = [d if j == k else p[k][j] * d for j in range(n)]
        new = []
        for i in range(n):
            if i == k:
                new.append(row)
            else:
                new.append(
                    [
                        -p[i][k] * d if j == k else p[i][j] - p[i][k] * row[j]
                        for j in range(n)
                    ]
                )
        p = new
    return p


def block_inverse(block, pivots, group=8):
    tiles = [block[8 * g : 8 * g + 8] for g in range(LANES // 8)]
    lane = lax.broadcasted_iota(jnp.int32, (8, LANES), 1)
    line = lax.broadcasted_iota(jnp.int32, (8, LANES), 0)
    for k in range(0, pivots, group):
        g, r = divmod(k, 8)
        cols = [
            [
                jnp.broadcast_to(t[:, k + j : k + j + 1], (8, LANES))
                for t in tiles
            ]
            for j in range(group)
        ]
        small = [
            [cols[j][g][r + i : r + i + 1] for j in range(group)]
            for i in range(group)
        ]
        small = small_inverse(small)
        rows = []
        for i in range(group):
            old = tiles[g][r + i : r + i + 1]
            old = jnp.where((lane[:1] >= k) & (lane[:1] < k + group), 0.0, old)
            rows.append(jnp.where(lane[:1] == k + i, 1.0, old))
        new_rows = []
        for i in range(group):
            total = small[i][0] * rows[0]
            for j in range(1, group):
                total = total + small[i][j] * rows[j]
            new_rows.append(jnp.broadcast_to(total, (8, LANES)))
        keep = (lane < k) | (lane >= k + group)
        for t in range(LANES // 8):
            value = jnp.where(keep, tiles[t], 0.0)
            for j in range(group):
                value = value - cols[j][t] * new_rows[j]
            if t == g:
                for i in range(group):
                    value = jnp.where(line == r + i, new_rows[i], value)
            tiles[t] = value
    return jnp.concatenate(tiles, 0)


def dot32(a, b):
    return jnp.dot(
        a, b, precision=lax.Precision.HIGHEST, preferred_element_type=F32
    )


def solve_kernel(
    packed_ref,
    feats_ref,
    index_ref,
    yield_ref,
    fitted_ref,
    spread_ref,
    resid_ref,
    system,
    base,
    high_ref,
    low_ref,
    fit,
):
    width, pixels = feats_ref.shape
    count = pl.cdiv(width, LANES)
    size = count * LANES
    blocks, offset = bands(width)
    scale = 1.0 / pixels
    line = lax.broadcasted_iota(jnp.int32, (LANES, LANES), 0)
    lane = lax.broadcasted_iota(jnp.int32, (LANES, LANES), 1)
    for i, j, height, at in blocks:
        value = packed_ref[at : at + height] * scale
        if height < LANES:
            value = jnp.concatenate(
                [value, jnp.zeros((LANES - height, LANES), F32)], 0
            )
        if i == j:
            diagonal = jnp.where(line < height, ridge_term, 1.0)
            value = value + jnp.where(line == lane, diagonal, 0.0)
        system[i * LANES : (i + 1) * LANES, j * LANES : (j + 1) * LANES] = value
        if i != j:
            system[j * LANES : (j + 1) * LANES, i * LANES : (i + 1) * LANES] = value.T

    base[...] = system[...]
    column = lax.broadcasted_iota(jnp.int32, (LANES, size), 1)
    wide_line = lax.broadcasted_iota(jnp.int32, (LANES, size), 0)

    def eliminate(k, pivots):
        at = k * LANES if isinstance(k, int) else pl.multiple_of(k * LANES, LANES)
        here = pl.ds(at, LANES)
        inverse = block_inverse(system[here, here], pivots)
        inside = (column >= at) & (column < at + LANES)
        unit = jnp.where(column == wide_line + at, 1.0, 0.0)
        right = dot32(inverse, jnp.where(inside, unit, system[here, :]))
        left = system[:, here]
        system[:, here] = jnp.zeros_like(left)
        system[...] -= dot32(left, right)
        system[here, :] = right

    full = width // LANES

    def body(k, _):
        eliminate(k, LANES)
        return 0

    lax.fori_loop(0, full, body, 0)
    if width % LANES:
        eliminate(full, width % LANES)

    rhs = jnp.concatenate(
        [packed_ref[offset + j : offset + j + 1] for j in range(count)], 1
    )
    rhs = jnp.broadcast_to(rhs * scale, (8, size))
    beta = dot32(rhs, system[...])
    beta = beta + dot32(rhs - dot32(beta, base[...]), system[...])
    beta = beta[:1, :width]
    inverse = system[:width, :width]
    upper = inverse.astype(BF16)
    a, b, d = (p.astype(F32) for p in split3(beta))
    row16 = lax.broadcasted_iota(jnp.int32, (16, width), 0)
    extra = jnp.where(row16 == 0, a, jnp.where(row16 == 1, b, jnp.where(row16 == 2, d, 0.0)))
    high_ref[...] = jnp.concatenate([upper, extra.astype(BF16)], 0)
    low_ref[...] = (inverse - upper.astype(F32)).astype(BF16)

    def step(c, _):
        at = pl.multiple_of(c * CHUNK, CHUNK)
        feats = feats_ref[:, pl.ds(at, CHUNK)]
        first = jnp.dot(high_ref[...], feats, preferred_element_type=F32)
        second = jnp.dot(low_ref[...], feats, preferred_element_type=F32)
        total = (first[:width] + second) * feats.astype(F32)
        spread_ref[:, pl.ds(at, CHUNK)] = jnp.sum(total, 0, keepdims=True) / width
        fitted = first[width : width + 1] + (
            first[width + 1 : width + 2] + first[width + 2 : width + 3]
        )
        fitted_ref[:, pl.ds(at, CHUNK)] = fitted
        for s in range(CHUNK // LANES):
            fit[pl.ds(c * (CHUNK // LANES) + s, 1), :] = fitted[
                :, s * LANES : (s + 1) * LANES
            ]
        return 0

    lax.fori_loop(0, pixels // CHUNK, step, 0)

    rows = pixels // LANES
    high, low = one_hots(index_ref[...], rows)
    low = jnp.where(low, 1.0, 0.0).astype(BF16)
    table = jnp.concatenate(split3(fit[...]), 0)
    found = jnp.dot(table, low, preferred_element_type=F32)
    found = found[:rows] + (found[rows : 2 * rows] + found[2 * rows :])
    value = jnp.sum(jnp.where(high, found, 0.0), 0, keepdims=True)
    resid_ref[...] = yield_ref[...] - value


PARAMS = pltpu.CompilerParams(vmem_limit_bytes=48 * 1024 * 1024)


def segments(index, yields, mask):
    shape = jax.ShapeDtypeStruct(mask.shape, F32)
    return pl.pallas_call(
        segment_kernel,
        out_shape=(shape, shape),
        compiler_params=PARAMS,
        cost_estimate=pl.CostEstimate(
            flops=2 * 128 * 128 * index.shape[1],
            bytes_accessed=16 * index.shape[1],
            transcendentals=0,
        ),
        name="segments",
    )(index, yields, mask)


def grams(feats, weight, product):
    width, pixels = feats.shape
    rows = bands(width)[1] + 8 * pl.cdiv(pl.cdiv(width, LANES), 8)
    return pl.pallas_call(
        gram_kernel,
        out_shape=jax.ShapeDtypeStruct((rows, LANES), F32),
        scratch_shapes=[pltpu.VMEM((width + 16, width), F32)],
        compiler_params=PARAMS,
        name="grams",
    )(feats, weight, product)


def solves(packed, feats, index, yields):
    width, pixels = feats.shape
    size = pl.cdiv(width, LANES) * LANES
    shape = jax.ShapeDtypeStruct((1, pixels), F32)
    return pl.pallas_call(
        solve_kernel,
        out_shape=(shape, shape, jax.ShapeDtypeStruct(yields.shape, F32)),
        scratch_shapes=[
            pltpu.VMEM((size, size), F32),
            pltpu.VMEM((size, size), F32),
            pltpu.VMEM((width + 16, width), BF16),
            pltpu.VMEM((width, width), BF16),
            pltpu.VMEM((pixels // LANES, LANES), F32),
        ],
        compiler_params=PARAMS,
        name="solves",
    )(packed, feats, index, yields)


def window_kernel(shape, own_ref, out_ref, landed, middle, send_sem, recv_sem):
    tiles, cols, dates = shape
    row = lax.axis_index("tiles")
    col = lax.axis_index("cols") * dates + lax.axis_index("dates")
    total = own_ref.shape[0]
    step = -(-total // (8 * PIECES)) * 8
    pieces = [pl.ds(at, min(step, total - at)) for at in range(0, total, step)]

    def place(c):
        return {"cols": c // dates, "dates": c % dates}

    links = (
        (row < tiles - 1, lambda: {"tiles": row + 1}, row > 0, lambda: {"tiles": row - 1}),
        (row > 0, lambda: {"tiles": row - 1}, row < tiles - 1, lambda: {"tiles": row + 1}),
        (col < cols * dates - 1, lambda: place(col + 1), col > 0, lambda: place(col - 1)),
        (col > 0, lambda: place(col - 1), col < cols * dates - 1, lambda: place(col + 1)),
    )

    def copy(d, i, source, device):
        return pltpu.make_async_remote_copy(
            src_ref=source.at[pieces[i]],
            dst_ref=landed.at[d, pieces[i]],
            send_sem=send_sem.at[d, i],
            recv_sem=recv_sem.at[d, i],
            device_id=device,
            device_id_type=pl.DeviceIdType.MESH,
        )

    barrier = pltpu.get_barrier_semaphore()
    for there, target, _, _ in links:

        @pl.when(there)
        def _(target=target):
            pl.semaphore_signal(
                barrier, inc=1, device_id=target(), device_id_type=pl.DeviceIdType.MESH
            )

    peers = sum(there.astype(jnp.int32) for there, _, _, _ in links)
    pl.semaphore_wait(barrier, peers)

    def send(d, i, source):
        there, target, _, _ = links[d]

        @pl.when(there)
        def _():
            copy(d, i, source, target()).start()

    def receive(d, i, source, into):
        _, _, there, origin = links[d]

        @pl.when(there)
        def _():
            copy(d, i, source, origin()).wait_recv()
            into[pieces[i]] += 0.5 * landed[d, pieces[i]]

    count = len(pieces)
    for i in range(count):
        send(0, i, own_ref)
        send(1, i, own_ref)
    for i in range(count):
        middle[pieces[i]] = own_ref[pieces[i]]
        receive(0, i, own_ref, middle)
        receive(1, i, own_ref, middle)
        send(2, i, middle)
        send(3, i, middle)
    for i in range(count):
        out_ref[pieces[i]] = middle[pieces[i]]
        receive(2, i, middle, out_ref)
        receive(3, i, middle, out_ref)
    for i in range(count):
        for d in range(4):
            there, target, _, _ = links[d]

            @pl.when(there)
            def _(d=d, i=i, target=target):
                copy(d, i, own_ref if d < 2 else middle, target()).wait_send()


def window(packed):
    shape = tuple(lax.axis_size(name) for name in ("tiles", "cols", "dates"))
    in_vmem = pl.BlockSpec(memory_space=pltpu.VMEM)
    return pl.pallas_call(
        functools.partial(window_kernel, shape),
        out_shape=jax.ShapeDtypeStruct(packed.shape, F32),
        in_specs=[in_vmem],
        out_specs=in_vmem,
        scratch_shapes=[
            pltpu.VMEM((4,) + packed.shape, F32),
            pltpu.VMEM(packed.shape, F32),
            pltpu.SemaphoreType.DMA((4, PIECES)),
            pltpu.SemaphoreType.DMA((4, PIECES)),
        ],
        compiler_params=pltpu.CompilerParams(
            collective_id=0,
            has_side_effects=True,
            vmem_limit_bytes=48 * 1024 * 1024,
        ),
        name="window",
    )(packed)


def on_device(imagery, pixel_mask, point_pixel, point_yield):
    whole = lax.all_to_all(imagery, "dates", split_axis=1, concat_axis=2, tiled=True)
    feats = whole[0, 0]
    pixels = feats.shape[1]
    index = point_pixel[0]
    yields = point_yield[0]
    mask = pixel_mask.reshape(pixels // LANES, LANES)
    weight, product = segments(index, yields, mask)
    packed = grams(feats, weight, product)
    packed = window(packed)
    fitted, spread, resid = solves(packed, feats, index, yields)
    return (fitted[None], spread[None], resid[None])


def solution(mesh):
    features = P(("groups", "tiles"), "cols", "dates", None)
    points = P(("groups", "tiles"), ("cols", "dates"), None)
    return jax.shard_map(
        on_device,
        mesh=mesh,
        in_specs=(features, points, points, points),
        out_specs=(points, points, points),
        check_vma=False,
    )
```
